256 devices in a mesh: shot: 4 (over x), space: 64 (over z, y, core).
Axes of the slice: x: 4, y: 4, z: 8, core: 2. Of those that a mesh axis runs over, the one named last changes fastest.
Arguments:
- model_velocity: float32 [2, 64, 4, 256, 128], P(None, 'space'), may hold values from 1.5 to 4.5
- first_tile: int32 [4], P('shot'), may hold values from 0 to 64
- src_weight: float32 [8, 256, 256], P('shot', 'space'), may hold values from -6 to 6
- src_depth: int32 [8, 256, 256], P('shot', 'space'), may hold values from 0 to 127
- wavelet: float32 [8, 4], P('shot'), may hold values from -0.6 to 0.6
- rec_depth: int32 [8, 256, 256], P('shot', 'space'), may hold values from 0 to 127
- residual: float32 [8, 4, 256, 256], P('shot', None, 'space'), may hold values from -0.6 to 0.6
Outputs:
- gradient: float32 [2, 64, 4, 256, 128], P(None, 'space', 'shot')
The draws below stay inside these ranges and needn't reach their ends.
Inputs may be any that keep to these rules, and one draw needn't show every extreme that they name: Group g's aperture is the 64 consecutive model tiles starting at first_tile[g].
All inputs are finite; a program needn't handle non-finite values.
Results may differ from the reference program's by a relative error of at most 0.0001.
Values sent between devices are 32-bit elements; how exact they have to be, the bound alone decides.
No kernel may reach another device: no remote copies, remote signals or barrier semaphores. Data moves between devices by JAX's collectives and lax.ppermute only.
A program may use at most 64 MiB of HBM per device.

```python
import jax
import jax.numpy as jnp
from jax import lax

CX = 4
CY = 256
CZ = 128
MT_DEV = 2
SHOTS_DEV = 2
STEPS = 4
GROUPS = 4
SHOTS = 8
NXA = 256
MODEL_TILES = 128
N_SPACE = 64


def plant(drawn, stream_key, low, top_value):
    dims = drawn.shape
    spot = [jax.random.randint(jax.random.fold_in(stream_key, axis), (), 0, dims[axis]) for axis in range(len(dims))]
    drawn = drawn.at[tuple(spot)].set(low)
    longest = dims.index(max(dims))
    spot[longest] = (spot[longest] + 1) % dims[longest]
    return drawn.at[tuple(spot)].set(top_value)


def block_scale(own_key, shape, shards, least, high):
    level = 1.0
    for dim, blocks in shards:
        draws = jax.random.uniform(jax.random.fold_in(jax.random.fold_in(own_key, 6), dim), (blocks,), jnp.float32, least / len(shards), high / len(shards))
        level = level * jnp.repeat(jnp.exp(draws), shape[dim] // blocks).reshape((-1,) + (1,) * (len(shape) - 1 - dim))
    return level


def scatter_about(rng, dims, spread, limit, shards=(), dtype=jnp.bfloat16):
    entries = spread * jax.random.normal(rng, dims, jnp.float32)
    if shards:
        entries = entries * block_scale(rng, dims, shards, -0.22, 0.18)
    return jnp.clip(entries, -limit, limit).astype(dtype)


def setup_inputs(seed: int = 0) -> dict:
    key_list = jax.random.split(jax.random.key(seed), 8)
    model_velocity = jnp.clip(1.5 + 3.0 * jax.random.uniform(key_list[0], (MT_DEV, N_SPACE, CX, CY, CZ), jnp.float32) ** block_scale(key_list[0], (MT_DEV, N_SPACE, CX, CY, CZ), ((1, 64),), -0.2, 0.2), 1.5, 4.5)
    first_tile = plant(jax.random.randint(key_list[1], (GROUPS,), 0, MODEL_TILES - N_SPACE + 1), jax.random.fold_in(key_list[1], 1), 0, MODEL_TILES - N_SPACE).astype(jnp.int32)
    src_weight = scatter_about(key_list[2], (SHOTS, NXA, CY), 1.0, 6.0, ((0, 4), (1, 64)), jnp.float32)
    src_depth = plant(jax.random.randint(key_list[3], (SHOTS, NXA, CY), 0, CZ), jax.random.fold_in(key_list[3], 1), 0, CZ - 1).astype(jnp.int32)
    wavelet = scatter_about(key_list[4], (SHOTS, STEPS), 0.1, 0.6, ((0, 4),), jnp.float32)
    rec_depth = plant(jax.random.randint(key_list[5], (SHOTS, NXA, CY), 0, CZ), jax.random.fold_in(key_list[5], 1), 0, CZ - 1).astype(jnp.int32)
    residual = scatter_about(key_list[6], (SHOTS, STEPS, NXA, CY), 0.1, 0.6, ((0, 4), (2, 64)), jnp.float32)
    return {"model_velocity": model_velocity, "first_tile": first_tile, "src_weight": src_weight, "src_depth": src_depth, "wavelet": wavelet, "rec_depth": rec_depth, "residual": residual}


COEFS = (-205.0 / 72.0, 8.0 / 5.0, -1.0 / 5.0, 8.0 / 315.0, -1.0 / 560.0)


def lap_local(padded_x):
    full = jnp.pad(padded_x, ((0, 0), (0, 0), (4, 4), (4, 4)))
    size_x = full.shape[1] - 8
    size_y = full.shape[2] - 8
    size_z = full.shape[3] - 8
    center = full[:, 4:4 + size_x, 4:4 + size_y, 4:4 + size_z]
    total = 3.0 * COEFS[0] * center
    for step in range(1, 5):
        beside_all = full[:, 4 + step:4 + step + size_x, 4:4 + size_y, 4:4 + size_z]
        beside_all = beside_all + full[:, 4 - step:4 - step + size_x, 4:4 + size_y, 4:4 + size_z]
        beside_all = beside_all + full[:, 4:4 + size_x, 4 + step:4 + step + size_y, 4:4 + size_z]
        beside_all = beside_all + full[:, 4:4 + size_x, 4 - step:4 - step + size_y, 4:4 + size_z]
        beside_all = beside_all + full[:, 4:4 + size_x, 4:4 + size_y, 4 + step:4 + step + size_z]
        beside_all = beside_all + full[:, 4:4 + size_x, 4:4 + size_y, 4 - step:4 - step + size_z]
        total = total + COEFS[step] * beside_all
    return total


def laplace(field):
    return lap_local(jnp.pad(field, ((0, 0), (4, 4), (0, 0), (0, 0))))


def group_image(velocity, src_weight, src_depth, wavelet, rec_depth, residual):
    coeff = (0.1 * velocity) ** 2
    depth = lax.broadcasted_iota(jnp.int32, (1, 1, 1, CZ), 3)
    source = jnp.where(depth == src_depth[..., None].astype(jnp.int32), src_weight[..., None], jnp.zeros((), jnp.float32))
    probe = jnp.where(depth == rec_depth[..., None].astype(jnp.int32), jnp.ones((), jnp.float32), jnp.zeros((), jnp.float32))
    start = jnp.zeros(source.shape, jnp.float32)

    def forward(carry, amplitude):
        before, now = carry
        lap_now = laplace(now)
        after = 2.0 * now - before + coeff * lap_now + amplitude[:, None, None, None] * source
        return (now, after), lap_now

    _, laps = lax.scan(forward, (start, start), jnp.transpose(wavelet))
    traces = jnp.moveaxis(jnp.flip(residual, 1), 1, 0)

    def adjoint(carry, items):
        before, now, image = carry
        lap_fwd, trace = items
        after = 2.0 * now - before + coeff * laplace(now) + trace[..., None] * probe
        return (now, after, image + after * lap_fwd), None

    (_, _, image), _ = lax.scan(adjoint, (start, start, start), (jnp.flip(laps, 0), traces))
    return 0.02 * velocity * jnp.sum(image, 0)


def reference(model_velocity, first_tile, src_weight, src_depth, wavelet, rec_depth, residual):
    flat_model = model_velocity.reshape(MODEL_TILES, CX, CY, CZ)
    total = jnp.zeros(flat_model.shape, jnp.float32)
    zero = jnp.zeros((), jnp.int32)
    for group in range(GROUPS):
        anchor = first_tile[group].astype(jnp.int32)
        tiles = lax.dynamic_slice(flat_model, (anchor, zero, zero, zero), (N_SPACE, CX, CY, CZ))
        velocity = tiles.reshape(NXA, CY, CZ)
        lo = group * SHOTS_DEV
        hi = lo + SHOTS_DEV
        image = group_image(velocity, src_weight[lo:hi], src_depth[lo:hi], wavelet[lo:hi], rec_depth[lo:hi], residual[lo:hi])
        current = lax.dynamic_slice(total, (anchor, zero, zero, zero), (N_SPACE, CX, CY, CZ))
        total = lax.dynamic_update_slice(total, current + image.reshape(N_SPACE, CX, CY, CZ), (anchor, zero, zero, zero))
    return total.reshape(MT_DEV, N_SPACE, CX, CY, CZ)
```

```python
import functools

import jax
import jax.numpy as jnp
import numpy as np
from jax import lax
from jax.experimental import pallas as pl
from jax.experimental.pallas import tpu as pltpu
from jax.sharding import PartitionSpec as P

COEFS = (-205.0 / 72.0, 8.0 / 5.0, -1.0 / 5.0, 8.0 / 315.0, -1.0 / 560.0)
CX, CY, CZ, STEPS = 4, 256, 128, 4
KINDS = 3 + STEPS
ROWS = KINDS * CX * (CY // 128)
WINDOW = 8
LAYERS = (WINDOW + 1) * CX


def band(size):
    apart = np.abs(np.arange(size)[:, None] - np.arange(size)[None, :])
    out = np.zeros((size, size), np.float64)
    for k in range(1, 5):
        out[apart == k] = COEFS[k]
    return out


def two_parts(matrix):
    high = matrix.astype(np.float32).astype(jnp.bfloat16)
    low = (matrix - high.astype(np.float64)).astype(np.float32).astype(jnp.bfloat16)
    return high, low


def ring(value, steps, axis="space"):
    count = lax.axis_size(axis)
    return lax.ppermute(value, axis, [(i, (i + steps) % count) for i in range(count)])


def swap(value):
    count = lax.axis_size("space")
    return lax.ppermute(value, "space", [(i, i ^ 1) for i in range(count)])


def kernel(
    numbers, amps, dy, dz, left, left_s, own, own_s, right, right_s, m2, m1, mid, p1, p2,
    out, comp, coeff, f1, f2, f3, lap1, lap2, lap3, yz, image, still,
):
    gap, odd, core = numbers[0], numbers[1], numbers[2]
    shift = 1 - odd
    depth_of = lax.broadcasted_iota(jnp.int32, (16, 128), 0).astype(jnp.float32)

    def base(w):
        return CX * w + jnp.where(w >= gap, CX, 0)

    for i, ref in enumerate((m2, m1, mid, p1)):
        comp[2 * i : 2 * i + 2] = ref[...]
    comp[8] = p2[...]
    still[...] = jnp.zeros_like(still)
    for field in (f1, f2, f3):
        field[pl.ds(CX * gap, CX)] = jnp.zeros((CX, CZ, CY), jnp.float32)
    for i, ref in enumerate((left, left_s, own, own_s, right, right_s)):
        w = jnp.bitwise_xor(i, core)

        def square(l, _, ref=ref, w=w):
            coeff[w, l] = (0.1 * ref[l].T) ** 2
            return 0

        lax.fori_loop(0, CX, square, 0)

    def row(w, kind, l, h):
        return comp[w + shift, pl.ds((kind * CX + l) * 2 + h, 1), :]

    def load(w, l, h, weight, place, amp):
        value = row(w, weight, l, h)
        if amp is not None:
            value = amps[amp] * value
        return value, row(w, place, l, h)

    def put(term, z):
        return jnp.where(depth_of + float(z) == term[1], term[0], 0.0)

    def first(weight, place, amp):
        def tile(w, _):
            b = base(w)
            for l in range(CX):
                for h in range(2):
                    term = load(w, l, h, weight, place, amp)
                    for z in range(0, CZ, 16):
                        f1[b + l, pl.ds(z, 16), pl.ds(128 * h, 128)] = put(term, z)
            return 0

        lax.fori_loop(0, WINDOW, tile, 0)

    def laplace(v, w, term_of, take):
        b = base(w)
        for l in range(CX):
            f = v[b + l]
            high = f.astype(jnp.bfloat16)
            low = (f - high.astype(jnp.float32)).astype(jnp.bfloat16)
            r = jnp.dot(jnp.concatenate([high, low, high], 1), dy[...], preferred_element_type=jnp.float32)
            r = r + jnp.dot(dz[...], jnp.concatenate([high, low, high], 0), preferred_element_type=jnp.float32)
            yz[l] = r
        for h in range(2):
            terms = [term_of(w, l, h) for l in range(CX)]
            for z in range(0, CZ, 16):
                at = (pl.ds(z, 16), pl.ds(128 * h, 128))
                x = [v[(b - 4 + i,) + at] for i in range(3 * CX)]
                for l in range(CX):
                    lap = yz[(l,) + at] + (3.0 * COEFS[0]) * x[4 + l]
                    for k in range(1, 5):
                        lap = lap + COEFS[k] * (x[4 + l + k] + x[4 + l - k])
                    take(w, b, l, at, x[4 + l], lap, put(terms[l], z) if terms[l] else None)

    def step(v, before, after, laps, low, weight, place, amp):
        def take(w, b, l, at, now, lap, term):
            if laps is not None:
                laps[(w - low, l) + at] = lap
            if after is not None:
                nxt = 2.0 * now + coeff[(w - 1, l) + at] * lap + term
                if before is not None:
                    nxt = nxt - before[(b + l,) + at]
                after[(b + l,) + at] = nxt

        def term_of(w, l, h):
            return load(w, l, h, weight, place, amp) if after is not None else None

        def tile(w, _):
            laplace(v, w, term_of, take)
            return 0

        lax.fori_loop(low, WINDOW - low, tile, 0)

    first(0, 1, 0)
    step(f1, None, f2, lap1, 1, 0, 1, 1)
    step(f2, f1, f3, lap2, 2, 0, 1, 2)
    step(f3, None, None, lap3, 3, 0, 1, None)
    first(3 + 3, 2, None)
    step(f1, None, f2, None, 1, 3 + 2, 2, None)
    step(f2, f1, f3, None, 2, 3 + 1, 2, None)
    for i, ref in enumerate((own, own_s)):
        w = 3 + jnp.bitwise_xor(i, core)

        def take(w, b, l, at, now, lap, term):
            w2 = f2[(b + l,) + at]
            w4 = 2.0 * now - w2 + coeff[(w - 1, l) + at] * lap + term
            total = f1[(b + l,) + at] * lap3[(w - 3, l) + at] + w2 * lap2[(w - 2, l) + at]
            image[(l,) + at] = total + now * lap1[(w - 1, l) + at] + w4 * still[...]

        def term_of(w, l, h):
            return load(w, l, h, 3, 2, None)

        laplace(f3, w, term_of, take)
        for l in range(CX):
            out[i, l] = 0.02 * ref[l] * image[l].T


def run_kernel(numbers, amps, tiles, surface):
    dyh, dyl = two_parts(band(CY))
    dzh, dzl = two_parts(band(CZ))
    dy = jnp.asarray(np.concatenate([dyh, dyh, dyl], 0))
    dz = jnp.asarray(np.concatenate([dzh, dzh, dzl], 1))
    vmem = pl.BlockSpec(memory_space=pltpu.VMEM)
    smem = pl.BlockSpec(memory_space=pltpu.SMEM)
    field = (CZ, CY)
    return pl.pallas_call(
        kernel,
        out_shape=jax.ShapeDtypeStruct((2, CX, CY, CZ), jnp.float32),
        in_specs=[smem, smem] + [vmem] * (2 + len(tiles) + len(surface)),
        out_specs=vmem,
        scratch_shapes=[
            pltpu.VMEM((10, ROWS, 128), jnp.float32),
            pltpu.VMEM((6, CX) + field, jnp.float32),
            pltpu.VMEM((LAYERS,) + field, jnp.float32),
            pltpu.VMEM((LAYERS,) + field, jnp.float32),
            pltpu.VMEM((LAYERS,) + field, jnp.float32),
            pltpu.VMEM((6, CX) + field, jnp.float32),
            pltpu.VMEM((4, CX) + field, jnp.float32),
            pltpu.VMEM((2, CX) + field, jnp.float32),
            pltpu.VMEM((CX,) + field, jnp.float32),
            pltpu.VMEM((CX,) + field, jnp.float32),
            pltpu.VMEM((16, 128), jnp.float32),
        ],
        compiler_params=pltpu.CompilerParams(vmem_limit_bytes=48 * 2**20),
    )(numbers, amps, dy, dz, *tiles, *surface)


def body(model_velocity, first_tile, src_weight, src_depth, wavelet, rec_depth, residual):
    width = lax.axis_size("space")
    groups = lax.axis_size("shot")
    group = lax.axis_index("shot")
    place = lax.axis_index("space")
    core = place % 2
    anchor = first_tile[0]

    def slot_of(o):
        return jnp.where(place >= o % width, o // width, o // width + 1)

    slot = slot_of(anchor)

    kinds = [src_weight, src_depth.astype(jnp.float32), rec_depth.astype(jnp.float32)]
    kinds += [residual[:, n] for n in range(STEPS)]
    surface = jnp.stack(kinds, 1).reshape(2, ROWS, 128)
    mine = lax.dynamic_index_in_dim(surface, core, 0, keepdims=False)
    theirs = swap(lax.dynamic_index_in_dim(surface, 1 - core, 0, keepdims=False))
    even = core == 0
    block = jnp.stack([jnp.where(even, mine, theirs), jnp.where(even, theirs, mine)])
    chips = (anchor // 2) % (width // 2)
    dy = chips % 4
    dz = chips // 4 + jnp.where(dy == 3, 1, 0)
    dy = jnp.where(dy == 3, -1, dy)
    dz = (dz + 3) % 8 - 3
    far = jnp.where(dz >= 2, 1, jnp.where(dz <= -2, -1, 0))
    near = dz - 3 * far

    def turn(value, digit, shifts):
        moved = [(d, ring(value, s)) for d, s in shifts]
        for d, m in moved:
            value = jnp.where(digit == d, m, value)
        return value

    block = turn(block, far, ((1, 24), (-1, -24)))
    block = turn(block, near, ((1, 8), (-1, -8)))
    block = turn(block, dy, ((1, 2), (2, 4), (-1, -2)))
    surfaces = (ring(block, 4), ring(block, 2), block, ring(block, -2), ring(block[0], -4))

    velocity = lax.dynamic_index_in_dim(model_velocity, slot, 0, keepdims=False)[0]
    left, right = ring(velocity, 2), ring(velocity, -2)
    tiles = (left, swap(left), velocity, swap(velocity), right, swap(right))

    cut = (anchor - (place - core - 3)) % width
    gap = jnp.where((cut >= 1) & (cut < WINDOW), cut, WINDOW)
    numbers = jnp.stack([gap, anchor % 2, core]).astype(jnp.int32)
    amps = lax.dynamic_index_in_dim(wavelet, core, 0, keepdims=False)
    part = run_kernel(numbers, amps, tiles, surfaces)
    local = part[0] + swap(part[1])

    anchors = lax.all_gather(first_tile, "shot", tiled=True)
    total = None
    for d in range(groups):
        piece = lax.dynamic_index_in_dim(local, (group + d) % groups, 0, keepdims=False)
        if d:
            piece = ring(piece, d, "shot")
        at = slot_of(anchors[(group - d) % groups])
        both = jnp.stack([jnp.where(at == s, piece, 0.0) for s in range(2)])
        total = both if total is None else total + both
    return total[:, None, None]


def solution(mesh):
    placed = (
        P(None, "space", None, None, None),
        P("shot"),
        P("shot", "space", None),
        P("shot", "space", None),
        P("shot", None),
        P("shot", "space", None),
        P("shot", None, "space", None),
    )
    return jax.shard_map(
        body,
        mesh=mesh,
        in_specs=placed,
        out_specs=P(None, "space", "shot", None, None),
        check_vma=False,
    )
```

```python
import functools

import jax
import jax.numpy as jnp
import numpy as np
from jax import lax
from jax.experimental import pallas as pl
from jax.experimental.pallas import tpu as pltpu
from jax.sharding import PartitionSpec as P

SCALE = 5040 / 128
COEFS = (None, 63.0, -7.875, 1.0, -0.0703125)
CENTER_Y, CENTER_Z = -336.0, -0.328125
CX, CY, CZ, STEPS = 4, 256, 128, 4
KINDS = 3 + STEPS
ROWS = KINDS * CX * (CY // 128)
WINDOW = 8
LAYERS = (WINDOW + 1) * CX


def band(size, center):
    apart = np.abs(np.arange(size)[:, None] - np.arange(size)[None, :])
    out = np.where(apart == 0, np.float32(center), np.float32(0))
    for k in range(1, 5):
        out[apart == k] = COEFS[k]
    return out.astype(jnp.bfloat16)


def ring(value, steps, axis="space"):
    count = lax.axis_size(axis)
    return lax.ppermute(value, axis, [(i, (i + steps) % count) for i in range(count)])


def either_way(value, steps):
    count = lax.axis_size("space")
    return lax.ppermute(
        value, "space", [(i, (i + (steps if i % 2 == 0 else -steps)) % count) for i in range(count)]
    )


def swap(value):
    count = lax.axis_size("space")
    return lax.ppermute(value, "space", [(i, i ^ 1) for i in range(count)])


def base_of(gap):
    return lambda w: CX * w + jnp.where(w >= gap, CX, 0)


def fetch(pairs, sems):
    copies = [pltpu.make_async_copy(src, dst, sems.at[i]) for i, (src, dst) in enumerate(pairs)]
    for copy in copies:
        copy.start()
    return copies


def fill_depths(depths):
    depths[...] = lax.broadcasted_iota(jnp.int32, (CZ, 128), 0).astype(jnp.float32)


def put(depths, term, z):
    return jnp.where(depths[pl.ds(z, 16), :] == term[1], term[0], 0.0)


def along(field, b, l, dy, dz, yz):
    f = field[b + l]
    high = f.astype(jnp.bfloat16)
    low = (f - high.astype(jnp.float32)).astype(jnp.bfloat16)
    r = jnp.dot(jnp.concatenate([high, low], 1), dy[...], preferred_element_type=jnp.float32)
    stack = jnp.concatenate([high, low], 0)
    yz[l] = r + jnp.dot(dz[...], stack, preferred_element_type=jnp.float32)


def across(field, b, n, yz, take):
    h, z = n // 8, 16 * (n % 8)
    at = (pl.ds(z, 16), pl.ds(128 * h, 128))
    x = [field[(b - 4 + i,) + at] for i in range(3 * CX)]
    for l in range(CX):
        lap = yz[(l,) + at]
        for k in range(1, 5):
            pair = x[4 + l + k] + x[4 + l - k]
            lap = lap + (pair if COEFS[k] == 1.0 else COEFS[k] * pair)
        take(l, h, z, at, x[4 + l], lap)


def sweep(u, w, low, high, place, dy, dz, yzu, yzw, take_u, take_w):
    def tile(t, _):
        b = place(t)
        for l in range(CX):
            along(u, b, l, dy, dz, yzu)
        take = take_u(t, b)
        for l in range(CX):
            along(w, b, l, dy, dz, yzw)
            for n in range(4 * l, 4 * l + 4):
                across(u, b, n, yzu, take)
        take = take_w(t, b)
        for n in range(16):
            across(w, b, n, yzw, take)
        return 0

    lax.fori_loop(low, high, tile, 0)


def first_kernel(
    numbers, amps, dy, dz, middle, a1, a2, a3, a4, others, lap_u, lap_w, comp,
    fu, fw, yzu, yzw, depths, sems,
):
    gap, start, core = numbers[0], numbers[1], numbers[2]
    base = base_of(gap)
    sign = 2 * core - 1
    pairs = [(middle.at[:, core], comp.at[pl.ds(8, 2)])]
    for i, ref in enumerate((a1, a2, a3, a4)):
        far = 2 * (i + 1) * sign
        pairs.append((ref.at[:, core], comp.at[pl.ds(8 + far, 2)]))
        pairs.append((others.at[i], comp.at[pl.ds(8 - far, 2)]))
    copies = fetch(pairs, sems)
    fill_depths(depths)
    for field in (fu, fw):
        field[pl.ds(CX * gap, CX)] = jnp.zeros((CX, CZ, CY), jnp.float32)
    for copy in copies:
        copy.wait()

    def row(w, kind, l, h):
        return comp[w + start, pl.ds((kind * CX + l) * 2 + h, 1), :]

    def fill(w, _):
        b = base(w)
        for l in range(CX):
            for h in range(2):
                u = (amps[0] * row(w, 0, l, h), row(w, 1, l, h))
                v = (row(w, 6, l, h), row(w, 2, l, h))
                for z in range(0, CZ, 16):
                    at = (b + l, pl.ds(z, 16), pl.ds(128 * h, 128))
                    fu[at] = put(depths, u, z)
                    fw[at] = put(depths, v, z)
        return 0

    lax.fori_loop(0, WINDOW, fill, 0)

    def keep(out):
        def at_tile(w, b):
            def take(l, h, z, at, now, lap):
                out[(w - 1, l) + at] = lap

            return take

        return at_tile

    sweep(fu, fw, 1, WINDOW - 1, base, dy, dz, yzu, yzw, keep(lap_u), keep(lap_w))


def second_kernel(
    numbers, amps, dy, dz, c0, c1, c2, c3, c4, c5, comp, lap_u, lap_w,
    out0, out1, coeff, u2, u3, w2, w3, lap2, lap3, yzu, yzw, image, depths, still, sems,
):
    gap, start, core = numbers[0], numbers[1], numbers[2]
    base = base_of(gap)
    tiles = (c0, c1, c2, c3, c4, c5)
    pairs = [(ref, coeff.at[jnp.bitwise_xor(i, core)]) for i, ref in enumerate(tiles)]
    copies = fetch(pairs, sems)
    fill_depths(depths)
    still[...] = jnp.zeros_like(still)
    for field in (u2, u3, w2, w3):
        field[pl.ds(CX * gap, CX)] = jnp.zeros((CX, CZ, CY), jnp.float32)
    for copy in copies:
        copy.wait()

    def row(w, kind, l, h):
        return comp[w + start, pl.ds((kind * CX + l) * 2 + h, 1), :]

    def source(w, amp):
        return {(l, h): (amp * row(w, 0, l, h), row(w, 1, l, h)) for l in range(CX) for h in range(2)}

    def trace(w, *scales):
        terms = {}
        for l in range(CX):
            for h in range(2):
                value = None
                for n, scale in scales:
                    r = row(w, 3 + n, l, h)
                    r = r if scale == 1 else scale * r
                    value = r if value is None else value + r
                terms[l, h] = (value, row(w, 2, l, h))
        return terms

    def second(w, _):
        b = base(w)
        su = source(w, 2.0 * amps[0] + amps[1])
        sw = trace(w, (3, 2.0), (2, 1))
        for l in range(CX):
            for h in range(2):
                for z in range(0, CZ, 16):
                    at = (pl.ds(z, 16), pl.ds(128 * h, 128))
                    c = coeff[(w - 1, l) + at]
                    u2[(b + l,) + at] = c * lap_u[(w - 1, l) + at] + put(depths, su[l, h], z)
                    w2[(b + l,) + at] = c * lap_w[(w - 1, l) + at] + put(depths, sw[l, h], z)
        return 0

    lax.fori_loop(1, WINDOW - 1, second, 0)

    def third_u(w, b):
        terms = source(w, amps[2] - amps[0])

        def take(l, h, z, at, now, lap):
            lap2[(w - 2, l) + at] = lap
            u3[(b + l,) + at] = 2.0 * now + coeff[(w - 1, l) + at] * lap + put(depths, terms[l, h], z)

        return take

    def third_w(w, b):
        terms = trace(w, (3, -1.0), (1, 1))

        def take(l, h, z, at, now, lap):
            w3[(b + l,) + at] = 2.0 * now + coeff[(w - 1, l) + at] * lap + put(depths, terms[l, h], z)

        return take

    sweep(u2, w2, 2, WINDOW - 2, base, dy, dz, yzu, yzw, third_u, third_w)

    def last_u(w, b):
        def take(l, h, z, at, now, lap):
            lap3[(w - 3, l) + at] = lap

        return take

    def last_w(w, b):
        ones, fours = trace(w, (3, 1)), trace(w, (0, 1))

        def take(l, h, z, at, now, lap):
            before = w2[(b + l,) + at]
            w4 = 2.0 * now - before + coeff[(w - 1, l) + at] * lap + put(depths, fours[l, h], z)
            total = put(depths, ones[l, h], z) * lap3[(w - 3, l) + at] + before * lap2[(w - 2, l) + at]
            image[(w - 3, l) + at] = total + now * lap_u[(w - 1, l) + at] + w4 * still[...]

        return take

    sweep(u3, w3, 3, WINDOW - 3, base, dy, dz, yzu, yzw, last_u, last_w)
    for l in range(CX):
        out0[l] = image[core, l].T
        out1[l] = image[1 - core, l].T


FIELD = (CZ, CY)
BLOCKS = 9


def matrices():
    dy, dz = band(CY, CENTER_Y), band(CZ, CENTER_Z)
    return jnp.asarray(np.concatenate([dy, dy], 0)), jnp.asarray(np.concatenate([dz, dz], 1))


def scratch(*lead):
    return pltpu.VMEM(lead + FIELD, jnp.float32)


def run_first(numbers, amps, surface):
    vmem = pl.BlockSpec(memory_space=pltpu.VMEM)
    smem = pl.BlockSpec(memory_space=pltpu.SMEM)
    anywhere = pl.BlockSpec(memory_space=pl.ANY)
    lap = jax.ShapeDtypeStruct((6, CX) + FIELD, jnp.float32)
    return pl.pallas_call(
        first_kernel,
        out_shape=(lap, lap, jax.ShapeDtypeStruct((2 * BLOCKS, ROWS, 128), jnp.float32)),
        in_specs=[smem, smem, vmem, vmem] + [anywhere] * 6,
        out_specs=(vmem, vmem, vmem),
        scratch_shapes=[
            scratch(LAYERS), scratch(LAYERS), scratch(CX), scratch(CX),
            pltpu.VMEM((CZ, 128), jnp.float32), pltpu.SemaphoreType.DMA((9,)),
        ],
        compiler_params=pltpu.CompilerParams(vmem_limit_bytes=28 * 2**20),
        cost_estimate=pl.CostEstimate(flops=10**6, bytes_accessed=2**20, transcendentals=0),
    )(numbers, amps, *matrices(), *surface)


def run_second(numbers, amps, coeffs, comp, lap_u, lap_w):
    vmem = pl.BlockSpec(memory_space=pltpu.VMEM)
    smem = pl.BlockSpec(memory_space=pltpu.SMEM)
    anywhere = pl.BlockSpec(memory_space=pl.ANY)
    out = jax.ShapeDtypeStruct((CX, CY, CZ), jnp.float32)
    return pl.pallas_call(
        second_kernel,
        out_shape=(out, out),
        in_specs=[smem, smem, vmem, vmem] + [anywhere] * 6 + [vmem] * 3,
        out_specs=(vmem, vmem),
        scratch_shapes=[
            scratch(6, CX),
            scratch(LAYERS), scratch(LAYERS), scratch(LAYERS), scratch(LAYERS),
            scratch(4, CX), scratch(2, CX), scratch(CX), scratch(CX), scratch(2, CX),
            pltpu.VMEM((CZ, 128), jnp.float32), pltpu.VMEM((16, 128), jnp.float32),
            pltpu.SemaphoreType.DMA((6,)),
        ],
        compiler_params=pltpu.CompilerParams(vmem_limit_bytes=40 * 2**20),
        cost_estimate=pl.CostEstimate(flops=9 * 10**9, bytes_accessed=12 * 2**20, transcendentals=0),
    )(numbers, amps, *matrices(), *coeffs, comp, lap_u, lap_w)


def body(model_velocity, first_tile, src_weight, src_depth, wavelet, rec_depth, residual):
    width = lax.axis_size("space")
    groups = lax.axis_size("shot")
    group = lax.axis_index("shot")
    place = lax.axis_index("space")
    core = place % 2
    anchor = first_tile[0]

    def slot_of(o):
        return jnp.where(place >= o % width, o // width, o // width + 1)

    slot = slot_of(anchor)

    velocity = lax.dynamic_index_in_dim(model_velocity, slot, 0, keepdims=False)[0]
    own = ((0.1 * velocity) ** 2 * (1.0 / SCALE)).transpose(0, 2, 1)

    kinds = [src_weight, src_depth.astype(jnp.float32), rec_depth.astype(jnp.float32)]
    kinds += [residual[:, n] for n in range(STEPS)]
    surface = jnp.stack(kinds, 1).reshape(2, ROWS, 128)
    first = core == 0

    def both(value):
        other = swap(value)
        return jnp.where(first, value, other), jnp.where(first, other, value)

    chips = (anchor // 2) % (width // 2)
    dy = chips % 4
    dz = chips // 4 + jnp.where(dy == 3, 1, 0)
    dy = jnp.where(dy == 3, -1, dy)
    dz = (dz + 3) % 8 - 3
    far = jnp.where(dz >= 2, 1, jnp.where(dz <= -2, -1, 0))
    near = dz - 3 * far

    def turn(value, digit, steps):
        up, down = both(either_way(value, steps))
        return jnp.where(digit == 1, up, jnp.where(digit == -1, down, value))

    block = jnp.stack(both(surface))
    block = turn(block, far, 24)
    block = turn(block, near, 8)

    ours = [either_way(block, 2 * q) for q in range(1, 5)]
    ours[3], own = lax.optimization_barrier((ours[3], own))
    left, right = ring(own, 2), ring(own, -2)
    others = jnp.stack([lax.dynamic_index_in_dim(value, 1 - core, 1, keepdims=False) for value in ours])
    blocks = [block] + ours + [swap(others)]
    cut = (anchor - (place - core - 3)) % width
    gap = jnp.where((cut >= 1) & (cut < WINDOW), cut, WINDOW)
    numbers = jnp.stack([gap, 5 - 2 * dy - anchor % 2, core]).astype(jnp.int32)
    amps = lax.dynamic_index_in_dim(wavelet, core, 0, keepdims=False)
    lap_u, lap_w, comp = run_first(numbers, amps, blocks)
    left, right, lap_u = lax.optimization_barrier((left, right, lap_u))

    coeffs = (left, swap(left), own, swap(own), right, swap(right))
    mine, theirs = run_second(numbers, amps, coeffs, comp, lap_u, lap_w)
    local = (0.02 / SCALE) * velocity * (mine + swap(theirs))

    flag = jnp.full((CX, 8, CZ), slot, jnp.int32).astype(jnp.float32)
    local = jnp.concatenate([local, flag], 1)
    total = None
    for d in range(groups):
        piece = lax.dynamic_index_in_dim(local, (group + d) % groups, 0, keepdims=False)
        if d:
            piece = ring(piece, d, "shot")
        at = piece[CY : CY + 1]
        both = jnp.stack([jnp.where(at == s, piece[:CY], 0.0) for s in range(2)])
        total = both if total is None else total + both
    return total[:, None, None]


def solution(mesh):
    placed = (
        P(None, "space", None, None, None),
        P("shot"),
        P("shot", "space", None),
        P("shot", "space", None),
        P("shot", None),
        P("shot", "space", None),
        P("shot", None, "space", None),
    )
    return jax.shard_map(
        body,
        mesh=mesh,
        in_specs=placed,
        out_specs=P(None, "space", "shot", None, None),
        check_vma=False,
    )
```

```python
import functools

import jax
import jax.numpy as jnp
import numpy as np
from jax import lax
from jax.experimental import pallas as pl
from jax.experimental.pallas import tpu as pltpu
from jax.sharding import PartitionSpec as P

SCALE = 5040 / 128
COEFS = (None, 63.0, -7.875, 1.0, -0.0703125)
CENTER_Y, CENTER_Z = -336.0, -0.328125
CX, CY, CZ, STEPS = 4, 256, 128, 4
KINDS = 3 + STEPS
ROWS = KINDS * CX * (CY // 128)
WINDOW = 8
LAYERS = (WINDOW + 1) * CX


def band(size, center):
    apart = np.abs(np.arange(size)[:, None] - np.arange(size)[None, :])
    out = np.where(apart == 0, np.float32(center), np.float32(0))
    for k in range(1, 5):
        out[apart == k] = COEFS[k]
    return out.astype(jnp.bfloat16)


def ring(value, steps, axis="space"):
    count = lax.axis_size(axis)
    return lax.ppermute(value, axis, [(i, (i + steps) % count) for i in range(count)])


def either_way(value, steps):
    count = lax.axis_size("space")
    return lax.ppermute(
        value, "space", [(i, (i + (steps if i % 2 == 0 else -steps)) % count) for i in range(count)]
    )


def swap(value):
    count = lax.axis_size("space")
    return lax.ppermute(value, "space", [(i, i ^ 1) for i in range(count)])


def base_of(gap):
    return lambda w: CX * w + jnp.where(w >= gap, CX, 0)


def fetch(pairs, sems):
    copies = [pltpu.make_async_copy(src, dst, sems.at[i]) for i, (src, dst) in enumerate(pairs)]
    for copy in copies:
        copy.start()
    return copies


def fill_depths(depths):
    depths[...] = lax.broadcasted_iota(jnp.int32, (CZ, 128), 0).astype(jnp.float32)


def put(depths, term, z):
    return jnp.where(depths[pl.ds(z, 16), :] == term[1], term[0], 0.0)


def along(field, b, l, dy, dz, yz):
    f = field[b + l]
    high = f.astype(jnp.bfloat16)
    low = (f - high.astype(jnp.float32)).astype(jnp.bfloat16)
    r = jnp.dot(jnp.concatenate([high, low], 1), dy[...], preferred_element_type=jnp.float32)
    stack = jnp.concatenate([high, low], 0)
    yz[l] = r + jnp.dot(dz[...], stack, preferred_element_type=jnp.float32)


def across(field, b, n, yz, take):
    h, z = n // 8, 16 * (n % 8)
    at = (pl.ds(z, 16), pl.ds(128 * h, 128))
    x = [field[(b - 4 + i,) + at] for i in range(3 * CX)]
    for l in range(CX):
        lap = yz[(l,) + at]
        for k in range(1, 5):
            pair = x[4 + l + k] + x[4 + l - k]
            lap = lap + (pair if COEFS[k] == 1.0 else COEFS[k] * pair)
        take(l, h, z, at, x[4 + l], lap)


def sweep(u, w, low, high, place, dy, dz, yzu, yzw, take_u, take_w):
    def tile(t, _):
        b = place(t)
        for l in range(CX):
            along(u, b, l, dy, dz, yzu)
        take = take_u(t, b)
        for l in range(CX):
            along(w, b, l, dy, dz, yzw)
            for n in range(4 * l, 4 * l + 4):
                across(u, b, n, yzu, take)
        take = take_w(t, b)
        for n in range(16):
            across(w, b, n, yzw, take)
        return 0

    lax.fori_loop(low, high, tile, 0)


def first_kernel(
    numbers, amps, dy, dz, middle, a1, a2, a3, a4, others, lap_u, lap_w, comp,
    fu, fw, yzu, yzw, depths, sems,
):
    gap, start, core = numbers[0], numbers[1], numbers[2]
    base = base_of(gap)
    sign = 2 * core - 1
    pairs = [(middle.at[:, core], comp.at[pl.ds(8, 2)])]
    for i, ref in enumerate((a1, a2, a3, a4)):
        far = 2 * (i + 1) * sign
        pairs.append((ref.at[:, core], comp.at[pl.ds(8 + far, 2)]))
        pairs.append((others.at[i], comp.at[pl.ds(8 - far, 2)]))
    copies = fetch(pairs, sems)
    fill_depths(depths)
    for field in (fu, fw):
        field[pl.ds(CX * gap, CX)] = jnp.zeros((CX, CZ, CY), jnp.float32)
    for copy in copies:
        copy.wait()

    def row(w, kind, l, h):
        return comp[w + start, pl.ds((kind * CX + l) * 2 + h, 1), :]

    def fill(w, _):
        b = base(w)
        for l in range(CX):
            for h in range(2):
                u = (amps[0] * row(w, 0, l, h), row(w, 1, l, h))
                v = (row(w, 6, l, h), row(w, 2, l, h))
                for z in range(0, CZ, 16):
                    at = (b + l, pl.ds(z, 16), pl.ds(128 * h, 128))
                    fu[at] = put(depths, u, z)
                    fw[at] = put(depths, v, z)
        return 0

    lax.fori_loop(0, WINDOW, fill, 0)

    def keep(out):
        def at_tile(w, b):
            def take(l, h, z, at, now, lap):
                out[(w - 1, l) + at] = lap

            return take

        return at_tile

    sweep(fu, fw, 1, WINDOW - 1, base, dy, dz, yzu, yzw, keep(lap_u), keep(lap_w))


def second_kernel(
    numbers, amps, dy, dz, c0, c1, c2, c3, c4, c5, comp, lap_u, lap_w,
    out0, out1, coeff, u2, u3, w2, w3, lap2, lap3, yzu, yzw, image, depths, still, sems,
):
    gap, start, core = numbers[0], numbers[1], numbers[2]
    base = base_of(gap)
    tiles = (c0, c1, c2, c3, c4, c5)
    pairs = [(ref, coeff.at[jnp.bitwise_xor(i, core)]) for i, ref in enumerate(tiles)]
    copies = fetch(pairs, sems)
    fill_depths(depths)
    still[...] = jnp.zeros_like(still)
    for field in (u2, u3, w2, w3):
        field[pl.ds(CX * gap, CX)] = jnp.zeros((CX, CZ, CY), jnp.float32)

    def row(w, kind, l, h):
        return comp[w + start, pl.ds((kind * CX + l) * 2 + h, 1), :]

    def source(w, amp):
        return {(l, h): (amp * row(w, 0, l, h), row(w, 1, l, h)) for l in range(CX) for h in range(2)}

    def trace(w, *scales):
        terms = {}
        for l in range(CX):
            for h in range(2):
                value = None
                for n, scale in scales:
                    r = row(w, 3 + n, l, h)
                    r = r if scale == 1 else scale * r
                    value = r if value is None else value + r
                terms[l, h] = (value, row(w, 2, l, h))
        return terms

    def second(w, _):
        b = base(w)
        su = source(w, 2.0 * amps[0] + amps[1])
        sw = trace(w, (3, 2.0), (2, 1))
        for l in range(CX):
            for h in range(2):
                for z in range(0, CZ, 16):
                    at = (pl.ds(z, 16), pl.ds(128 * h, 128))
                    c = coeff[(w - 1, l) + at]
                    u2[(b + l,) + at] = c * lap_u[(w - 1, l) + at] + put(depths, su[l, h], z)
                    w2[(b + l,) + at] = c * lap_w[(w - 1, l) + at] + put(depths, sw[l, h], z)
        return 0

    for low in (3, 1, 5):
        for copy in copies[low - 1 : low + 1]:
            copy.wait()
        lax.fori_loop(low, low + 2, second, 0)

    def third_u(w, b):
        terms = source(w, amps[2] - amps[0])

        def take(l, h, z, at, now, lap):
            lap2[(w - 2, l) + at] = lap
            u3[(b + l,) + at] = 2.0 * now + coeff[(w - 1, l) + at] * lap + put(depths, terms[l, h], z)

        return take

    def third_w(w, b):
        terms = trace(w, (3, -1.0), (1, 1))

        def take(l, h, z, at, now, lap):
            w3[(b + l,) + at] = 2.0 * now + coeff[(w - 1, l) + at] * lap + put(depths, terms[l, h], z)

        return take

    sweep(u2, w2, 2, WINDOW - 2, base, dy, dz, yzu, yzw, third_u, third_w)

    def last_u(w, b):
        def take(l, h, z, at, now, lap):
            lap3[(w - 3, l) + at] = lap

        return take

    def last_w(w, b):
        ones, fours = trace(w, (3, 1)), trace(w, (0, 1))

        def take(l, h, z, at, now, lap):
            before = w2[(b + l,) + at]
            w4 = 2.0 * now - before + coeff[(w - 1, l) + at] * lap + put(depths, fours[l, h], z)
            total = put(depths, ones[l, h], z) * lap3[(w - 3, l) + at] + before * lap2[(w - 2, l) + at]
            image[(w - 3, l) + at] = total + now * lap_u[(w - 1, l) + at] + w4 * still[...]

        return take

    sweep(u3, w3, 3, WINDOW - 3, base, dy, dz, yzu, yzw, last_u, last_w)
    for l in range(CX):
        out0[l] = image[core, l]
        out1[l] = image[1 - core, l]


FIELD = (CZ, CY)
BLOCKS = 9


def matrices():
    dy, dz = band(CY, CENTER_Y), band(CZ, CENTER_Z)
    return jnp.asarray(np.concatenate([dy, dy], 0)), jnp.asarray(np.concatenate([dz, dz], 1))


def scratch(*lead):
    return pltpu.VMEM(lead + FIELD, jnp.float32)


def run_first(numbers, amps, surface):
    vmem = pl.BlockSpec(memory_space=pltpu.VMEM)
    smem = pl.BlockSpec(memory_space=pltpu.SMEM)
    anywhere = pl.BlockSpec(memory_space=pl.ANY)
    lap = jax.ShapeDtypeStruct((6, CX) + FIELD, jnp.float32)
    return pl.pallas_call(
        first_kernel,
        out_shape=(lap, lap, jax.ShapeDtypeStruct((2 * BLOCKS, ROWS, 128), jnp.float32)),
        in_specs=[smem, smem, vmem, vmem] + [anywhere] * 6,
        out_specs=(vmem, vmem, vmem),
        scratch_shapes=[
            scratch(LAYERS), scratch(LAYERS), scratch(CX), scratch(CX),
            pltpu.VMEM((CZ, 128), jnp.float32), pltpu.SemaphoreType.DMA((9,)),
        ],
        compiler_params=pltpu.CompilerParams(vmem_limit_bytes=28 * 2**20),
        cost_estimate=pl.CostEstimate(flops=10**6, bytes_accessed=2**20, transcendentals=0),
    )(numbers, amps, *matrices(), *surface)


def run_second(numbers, amps, coeffs, comp, lap_u, lap_w):
    vmem = pl.BlockSpec(memory_space=pltpu.VMEM)
    smem = pl.BlockSpec(memory_space=pltpu.SMEM)
    anywhere = pl.BlockSpec(memory_space=pl.ANY)
    out = jax.ShapeDtypeStruct((CX,) + FIELD, jnp.float32)
    return pl.pallas_call(
        second_kernel,
        out_shape=(out, out),
        in_specs=[smem, smem, vmem, vmem] + [anywhere] * 6 + [vmem] * 3,
        out_specs=(vmem, vmem),
        scratch_shapes=[
            scratch(6, CX),
            scratch(LAYERS), scratch(LAYERS), scratch(LAYERS), scratch(LAYERS),
            scratch(4, CX), scratch(2, CX), scratch(CX), scratch(CX), scratch(2, CX),
            pltpu.VMEM((CZ, 128), jnp.float32), pltpu.VMEM((16, 128), jnp.float32),
            pltpu.SemaphoreType.DMA((6,)),
        ],
        compiler_params=pltpu.CompilerParams(vmem_limit_bytes=40 * 2**20),
        cost_estimate=pl.CostEstimate(flops=9 * 10**9, bytes_accessed=12 * 2**20, transcendentals=0),
    )(numbers, amps, *matrices(), *coeffs, comp, lap_u, lap_w)


def body(model_velocity, first_tile, src_weight, src_depth, wavelet, rec_depth, residual):
    width = lax.axis_size("space")
    groups = lax.axis_size("shot")
    group = lax.axis_index("shot")
    place = lax.axis_index("space")
    core = place % 2
    anchor = first_tile[0]

    def slot_of(o):
        return jnp.where(place >= o % width, o // width, o // width + 1)

    slot = slot_of(anchor)

    velocity = lax.dynamic_index_in_dim(model_velocity, slot, 0, keepdims=False)[0]
    own = ((0.1 * velocity) ** 2 * (1.0 / SCALE)).transpose(0, 2, 1)

    kinds = [src_weight, src_depth.astype(jnp.float32), rec_depth.astype(jnp.float32)]
    kinds += [residual[:, n] for n in range(STEPS)]
    surface = jnp.stack(kinds, 1).reshape(2, ROWS, 128)
    first = core == 0

    def both(value):
        other = swap(value)
        return jnp.where(first, value, other), jnp.where(first, other, value)

    chips = (anchor // 2) % (width // 2)
    dy = chips % 4
    dz = chips // 4 + jnp.where(dy == 3, 1, 0)
    dy = jnp.where(dy == 3, -1, dy)
    dz = (dz + 3) % 8 - 3
    far = jnp.where(dz >= 2, 1, jnp.where(dz <= -2, -1, 0))
    near = dz - 3 * far

    def turn(value, digit, steps):
        up, down = both(either_way(value, steps))
        return jnp.where(digit == 1, up, jnp.where(digit == -1, down, value))

    block = jnp.stack(both(surface))
    block = turn(block, far, 24)
    block = turn(block, near, 8)

    ours = [either_way(block, 2 * q) for q in range(1, 5)]
    ours[3], own = lax.optimization_barrier((ours[3], own))
    left, right = ring(own, 2), ring(own, -2)
    others = jnp.stack([lax.dynamic_index_in_dim(value, 1 - core, 1, keepdims=False) for value in ours])
    blocks = [block] + ours + [swap(others)]
    cut = (anchor - (place - core - 3)) % width
    gap = jnp.where((cut >= 1) & (cut < WINDOW), cut, WINDOW)
    numbers = jnp.stack([gap, 5 - 2 * dy - anchor % 2, core]).astype(jnp.int32)
    amps = lax.dynamic_index_in_dim(wavelet, core, 0, keepdims=False)
    lap_u, lap_w, comp = run_first(numbers, amps, blocks)
    left, right, lap_u = lax.optimization_barrier((left, right, lap_u))

    coeffs = (left, swap(left), own, swap(own), right, swap(right))
    mine, theirs = run_second(numbers, amps, coeffs, comp, lap_u, lap_w)
    local = (0.02 / SCALE) * velocity * (mine + swap(theirs)).transpose(0, 2, 1)

    flag = jnp.full((CX, 8, CZ), slot, jnp.int32).astype(jnp.float32)
    local = jnp.concatenate([local, flag], 1)
    total = None
    for d in range(groups):
        piece = lax.dynamic_index_in_dim(local, (group + d) % groups, 0, keepdims=False)
        if d:
            piece = ring(piece, d, "shot")
        at = piece[CY : CY + 1]
        both = jnp.stack([jnp.where(at == s, piece[:CY], 0.0) for s in range(2)])
        total = both if total is None else total + both
    return total[:, None, None]


def solution(mesh):
    placed = (
        P(None, "space", None, None, None),
        P("shot"),
        P("shot", "space", None),
        P("shot", "space", None),
        P("shot", None),
        P("shot", "space", None),
        P("shot", None, "space", None),
    )
    return jax.shard_map(
        body,
        mesh=mesh,
        in_specs=placed,
        out_specs=P(None, "space", "shot", None, None),
        check_vma=False,
    )
```

```python
import functools

import jax
import jax.numpy as jnp
import numpy as np
from jax import lax
from jax.experimental import pallas as pl
from jax.experimental.pallas import tpu as pltpu
from jax.sharding import PartitionSpec as P

SCALE = 5040 / 128
COEFS = (None, 63.0, -7.875, 1.0, -0.0703125)
CENTER_Y, CENTER_Z = -336.0, -0.328125
CX, CY, CZ, STEPS = 4, 256, 128, 4
KINDS = 3 + STEPS
ROWS = KINDS * CX * (CY // 128)
WINDOW = 8
LAYERS = (WINDOW + 1) * CX


def band(size, center):
    apart = np.abs(np.arange(size)[:, None] - np.arange(size)[None, :])
    out = np.where(apart == 0, np.float32(center), np.float32(0))
    for k in range(1, 5):
        out[apart == k] = COEFS[k]
    return out.astype(jnp.bfloat16)


def ring(value, steps, axis="space"):
    count = lax.axis_size(axis)
    return lax.ppermute(value, axis, [(i, (i + steps) % count) for i in range(count)])


def either_way(value, steps):
    count = lax.axis_size("space")
    return lax.ppermute(
        value, "space", [(i, (i + (steps if i % 2 == 0 else -steps)) % count) for i in range(count)]
    )


def swap(value):
    count = lax.axis_size("space")
    return lax.ppermute(value, "space", [(i, i ^ 1) for i in range(count)])


def base_of(gap):
    return lambda w: CX * w + jnp.where(w >= gap, CX, 0)


def fetch(pairs, sems):
    copies = [pltpu.make_async_copy(src, dst, sems.at[i]) for i, (src, dst) in enumerate(pairs)]
    for copy in copies:
        copy.start()
    return copies


def fill_depths(depths):
    depths[...] = lax.broadcasted_iota(jnp.int32, (CZ, 128), 0).astype(jnp.float32)


def put(depths, term, z):
    return jnp.where(depths[pl.ds(z, 16), :] == term[1], term[0], 0.0)


def along(field, b, l, dy, dz, yz):
    f = field[b + l]
    high = f.astype(jnp.bfloat16)
    low = (f - high.astype(jnp.float32)).astype(jnp.bfloat16)
    r = jnp.dot(jnp.concatenate([high, low], 1), dy[...], preferred_element_type=jnp.float32)
    stack = jnp.concatenate([high, low], 0)
    yz[l] = r + jnp.dot(dz[...], stack, preferred_element_type=jnp.float32)


def across(field, b, n, yz, take):
    h, z = n // 8, 16 * (n % 8)
    at = (pl.ds(z, 16), pl.ds(128 * h, 128))
    x = [field[(b - 4 + i,) + at] for i in range(3 * CX)]
    for l in range(CX):
        lap = yz[(l,) + at]
        for k in range(1, 5):
            pair = x[4 + l + k] + x[4 + l - k]
            lap = lap + (pair if COEFS[k] == 1.0 else COEFS[k] * pair)
        take(l, h, z, at, x[4 + l], lap)


def sweep(u, w, low, high, place, dy, dz, yzu, yzw, take_u, take_w):
    def tile(t, _):
        b = place(t)
        for l in range(CX):
            along(u, b, l, dy, dz, yzu)
        take = take_u(t, b)
        for l in range(CX):
            along(w, b, l, dy, dz, yzw)
            for n in range(4 * l, 4 * l + 4):
                across(u, b, n, yzu, take)
        take = take_w(t, b)
        for n in range(16):
            across(w, b, n, yzw, take)
        return 0

    lax.fori_loop(low, high, tile, 0)


def first_kernel(
    numbers, amps, dy, dz, middle, a1, a2, a3, a4, others, lap_u, lap_w, comp,
    fu, fw, yzu, yzw, depths, sems,
):
    gap, start, core = numbers[0], numbers[1], numbers[2]
    base = base_of(gap)
    sign = 2 * core - 1
    pairs = [(middle.at[:, core], comp.at[pl.ds(8, 2)])]
    for i, ref in enumerate((a1, a2, a3, a4)):
        far = 2 * (i + 1) * sign
        pairs.append((ref.at[:, core], comp.at[pl.ds(8 + far, 2)]))
        pairs.append((others.at[i], comp.at[pl.ds(8 - far, 2)]))
    copies = fetch(pairs, sems)
    fill_depths(depths)
    for field in (fu, fw):
        field[pl.ds(CX * gap, CX)] = jnp.zeros((CX, CZ, CY), jnp.float32)
    for copy in copies:
        copy.wait()

    def row(w, kind, l, h):
        return comp[w + start, pl.ds((kind * CX + l) * 2 + h, 1), :]

    def fill(w, _):
        b = base(w)
        for l in range(CX):
            for h in range(2):
                u = (amps[0] * row(w, 0, l, h), row(w, 1, l, h))
                v = (row(w, 6, l, h), row(w, 2, l, h))
                for z in range(0, CZ, 16):
                    at = (b + l, pl.ds(z, 16), pl.ds(128 * h, 128))
                    fu[at] = put(depths, u, z)
                    fw[at] = put(depths, v, z)
        return 0

    lax.fori_loop(0, WINDOW, fill, 0)

    def keep(out):
        def at_tile(w, b):
            def take(l, h, z, at, now, lap):
                out[(w - 1, l) + at] = lap

            return take

        return at_tile

    sweep(fu, fw, 1, WINDOW - 1, base, dy, dz, yzu, yzw, keep(lap_u), keep(lap_w))


def second_kernel(
    numbers, amps, dy, dz, c0, c1, c2, c3, c4, c5, comp, lap_u, lap_w,
    out0, out1, coeff, u2, u3, w2, w3, lap2, lap3, yzu, yzw, image, depths, still, sems,
):
    gap, start, core = numbers[0], numbers[1], numbers[2]
    base = base_of(gap)
    tiles = (c0, c1, c2, c3, c4, c5)
    pairs = [(ref, coeff.at[jnp.bitwise_xor(i, core)]) for i, ref in enumerate(tiles)]
    copies = fetch(pairs, sems)
    fill_depths(depths)
    still[...] = jnp.zeros_like(still)
    for field in (u2, u3, w2, w3):
        field[pl.ds(CX * gap, CX)] = jnp.zeros((CX, CZ, CY), jnp.float32)

    def row(w, kind, l, h):
        return comp[w + start, pl.ds((kind * CX + l) * 2 + h, 1), :]

    def source(w, amp):
        return {(l, h): (amp * row(w, 0, l, h), row(w, 1, l, h)) for l in range(CX) for h in range(2)}

    def trace(w, *scales):
        terms = {}
        for l in range(CX):
            for h in range(2):
                value = None
                for n, scale in scales:
                    r = row(w, 3 + n, l, h)
                    r = r if scale == 1 else scale * r
                    value = r if value is None else value + r
                terms[l, h] = (value, row(w, 2, l, h))
        return terms

    def second(w, _):
        b = base(w)
        su = source(w, 2.0 * amps[0] + amps[1])
        sw = trace(w, (3, 2.0), (2, 1))
        for l in range(CX):
            for h in range(2):
                for z in range(0, CZ, 16):
                    at = (pl.ds(z, 16), pl.ds(128 * h, 128))
                    c = coeff[(w - 1, l) + at]
                    u2[(b + l,) + at] = c * lap_u[(w - 1, l) + at] + put(depths, su[l, h], z)
                    w2[(b + l,) + at] = c * lap_w[(w - 1, l) + at] + put(depths, sw[l, h], z)
        return 0

    for low in (3, 1, 5):
        for copy in copies[low - 1 : low + 1]:
            copy.wait()
        lax.fori_loop(low, low + 2, second, 0)

    def third_u(w, b):
        terms = source(w, amps[2] - amps[0])

        def take(l, h, z, at, now, lap):
            lap2[(w - 2, l) + at] = lap
            u3[(b + l,) + at] = 2.0 * now + coeff[(w - 1, l) + at] * lap + put(depths, terms[l, h], z)

        return take

    def third_w(w, b):
        terms = trace(w, (3, -1.0), (1, 1))

        def take(l, h, z, at, now, lap):
            w3[(b + l,) + at] = 2.0 * now + coeff[(w - 1, l) + at] * lap + put(depths, terms[l, h], z)

        return take

    sweep(u2, w2, 2, WINDOW - 2, base, dy, dz, yzu, yzw, third_u, third_w)

    def last_u(w, b):
        def take(l, h, z, at, now, lap):
            lap3[(w - 3, l) + at] = lap

        return take

    def last_w(w, b):
        ones, fours = trace(w, (3, 1)), trace(w, (0, 1))

        def take(l, h, z, at, now, lap):
            before = w2[(b + l,) + at]
            w4 = 2.0 * now - before + coeff[(w - 1, l) + at] * lap + put(depths, fours[l, h], z)
            total = put(depths, ones[l, h], z) * lap3[(w - 3, l) + at] + before * lap2[(w - 2, l) + at]
            image[(w - 3, l) + at] = total + now * lap_u[(w - 1, l) + at] + w4 * still[...]

        return take

    sweep(u3, w3, 3, WINDOW - 3, base, dy, dz, yzu, yzw, last_u, last_w)
    for l in range(CX):
        out0[l] = image[core, l]
        out1[l] = image[1 - core, l]


FIELD = (CZ, CY)
BLOCKS = 9


def matrices():
    dy, dz = band(CY, CENTER_Y), band(CZ, CENTER_Z)
    return jnp.asarray(np.concatenate([dy, dy], 0)), jnp.asarray(np.concatenate([dz, dz], 1))


def scratch(*lead):
    return pltpu.VMEM(lead + FIELD, jnp.float32)


def run_first(numbers, amps, surface):
    vmem = pl.BlockSpec(memory_space=pltpu.VMEM)
    smem = pl.BlockSpec(memory_space=pltpu.SMEM)
    anywhere = pl.BlockSpec(memory_space=pl.ANY)
    lap = jax.ShapeDtypeStruct((6, CX) + FIELD, jnp.float32)
    return pl.pallas_call(
        first_kernel,
        out_shape=(lap, lap, jax.ShapeDtypeStruct((2 * BLOCKS, ROWS, 128), jnp.float32)),
        in_specs=[smem, smem, vmem, vmem] + [anywhere] * 6,
        out_specs=(vmem, vmem, vmem),
        scratch_shapes=[
            scratch(LAYERS), scratch(LAYERS), scratch(CX), scratch(CX),
            pltpu.VMEM((CZ, 128), jnp.float32), pltpu.SemaphoreType.DMA((9,)),
        ],
        compiler_params=pltpu.CompilerParams(vmem_limit_bytes=28 * 2**20),
        cost_estimate=pl.CostEstimate(flops=10**6, bytes_accessed=2**20, transcendentals=0),
    )(numbers, amps, *matrices(), *surface)


def run_second(numbers, amps, coeffs, comp, lap_u, lap_w):
    vmem = pl.BlockSpec(memory_space=pltpu.VMEM)
    smem = pl.BlockSpec(memory_space=pltpu.SMEM)
    anywhere = pl.BlockSpec(memory_space=pl.ANY)
    out = jax.ShapeDtypeStruct((CX,) + FIELD, jnp.float32)
    return pl.pallas_call(
        second_kernel,
        out_shape=(out, out),
        in_specs=[smem, smem, vmem, vmem] + [anywhere] * 6 + [vmem] * 3,
        out_specs=(vmem, vmem),
        scratch_shapes=[
            scratch(6, CX),
            scratch(LAYERS), scratch(LAYERS), scratch(LAYERS), scratch(LAYERS),
            scratch(4, CX), scratch(2, CX), scratch(CX), scratch(CX), scratch(2, CX),
            pltpu.VMEM((CZ, 128), jnp.float32), pltpu.VMEM((16, 128), jnp.float32),
            pltpu.SemaphoreType.DMA((6,)),
        ],
        compiler_params=pltpu.CompilerParams(vmem_limit_bytes=40 * 2**20),
        cost_estimate=pl.CostEstimate(flops=9 * 10**9, bytes_accessed=12 * 2**20, transcendentals=0),
    )(numbers, amps, *matrices(), *coeffs, comp, lap_u, lap_w)


def body(model_velocity, first_tile, src_weight, src_depth, wavelet, rec_depth, residual):
    width = lax.axis_size("space")
    groups = lax.axis_size("shot")
    group = lax.axis_index("shot")
    place = lax.axis_index("space")
    core = place % 2
    anchor = first_tile[0]

    def slot_of(o):
        return jnp.where(place >= o % width, o // width, o // width + 1)

    slot = slot_of(anchor)

    velocity = lax.dynamic_index_in_dim(model_velocity, slot, 0, keepdims=False)[0]
    own = ((0.1 * velocity) ** 2 * (1.0 / SCALE)).transpose(0, 2, 1)

    kinds = [src_weight, src_depth.astype(jnp.float32), rec_depth.astype(jnp.float32)]
    kinds += [residual[:, n] for n in range(STEPS)]
    surface = jnp.stack(kinds, 1).reshape(2, ROWS, 128)
    first = core == 0

    def both(value):
        other = swap(value)
        return jnp.where(first, value, other), jnp.where(first, other, value)

    chips = (anchor // 2) % (width // 2)
    dy = chips % 4
    dz = chips // 4 + jnp.where(dy == 3, 1, 0)
    dy = jnp.where(dy == 3, -1, dy)
    dz = (dz + 3) % 8 - 3
    far = jnp.where(dz >= 2, 1, jnp.where(dz <= -2, -1, 0))
    near = dz - 3 * far

    def turn(value, digit, steps):
        up, down = both(either_way(value, steps))
        return jnp.where(digit == 1, up, jnp.where(digit == -1, down, value))

    block = jnp.stack(both(surface))
    block = turn(block, far, 24)
    block = turn(block, near, 8)

    ours = [either_way(block, 2 * q) for q in range(1, 5)]
    ours[3], own = lax.optimization_barrier((ours[3], own))
    left, right = ring(own, 2), ring(own, -2)
    others = jnp.stack([lax.dynamic_index_in_dim(value, 1 - core, 1, keepdims=False) for value in ours])
    blocks = [block] + ours + [swap(others)]
    cut = (anchor - (place - core - 3)) % width
    gap = jnp.where((cut >= 1) & (cut < WINDOW), cut, WINDOW)
    numbers = jnp.stack([gap, 5 - 2 * dy - anchor % 2, core]).astype(jnp.int32)
    amps = lax.dynamic_index_in_dim(wavelet, core, 0, keepdims=False)
    lap_u, lap_w, comp = run_first(numbers, amps, blocks)
    left, right, lap_u = lax.optimization_barrier((left, right, lap_u))

    coeffs = (left, swap(left), own, swap(own), right, swap(right))
    mine, theirs = run_second(numbers, amps, coeffs, comp, lap_u, lap_w)
    local = (0.02 / SCALE) * velocity * (mine + swap(theirs)).transpose(0, 2, 1)

    flag = jnp.full((CX, 8, CZ), slot, jnp.int32).astype(jnp.float32)
    local = jnp.concatenate([local, flag], 1)
    def layer(d):
        return lax.dynamic_index_in_dim(local, (group + d) % groups, 0, keepdims=False)

    half = CY // 2
    opposite = layer(2)
    low = jnp.concatenate([opposite[:half], opposite[CY:]], 0)
    high = jnp.concatenate([opposite[half:CY], opposite[CY:]], 0)
    up = ring(jnp.concatenate([layer(1), low], 0), 1, "shot")
    down = ring(jnp.concatenate([layer(3), high], 0), -1, "shot")
    low, high = ring(up[CY + 8 :], 1, "shot"), ring(down[CY + 8 :], -1, "shot")
    far = jnp.concatenate([low[:half], high], 0)
    total = None
    for piece in (layer(0), up[: CY + 8], down[: CY + 8], far):
        at = piece[CY : CY + 1]
        both = jnp.stack([jnp.where(at == s, piece[:CY], 0.0) for s in range(2)])
        total = both if total is None else total + both
    return total[:, None, None]


def solution(mesh):
    placed = (
        P(None, "space", None, None, None),
        P("shot"),
        P("shot", "space", None),
        P("shot", "space", None),
        P("shot", None),
        P("shot", "space", None),
        P("shot", None, "space", None),
    )
    return jax.shard_map(
        body,
        mesh=mesh,
        in_specs=placed,
        out_specs=P(None, "space", "shot", None, None),
        check_vma=False,
    )
```
